32 devices in a mesh: member: 4 (over z), band: 8 (over y, x, core).
Axes of the slice: x: 2, y: 2, z: 4, core: 2. Of those that a mesh axis runs over, the one named last changes fastest.
Arguments:
- codes: int32 [64, 96, 6, 352], P('member', 'band'), may hold values from -127 to 127
- exponents: int32 [64, 96, 6], P('member', 'band'), may hold values from -8 to -4
- centers: float32 [6, 256], replicated, may hold values from -3 to 3
- widths: float32 [6], replicated, may hold values from 0.01 to 0.03
Outputs:
- smoothed: bfloat16 [96, 6, 352, 256], P('band', None, 'member')
The draws below stay inside these ranges and needn't reach their ends.
All inputs are finite; a program needn't handle non-finite values.
Results may differ from the reference program's by a relative error of at most 0.0034.
Values may be sent and summed in bfloat16 or wider, within the bound.
A program may use at most 64 MiB of HBM per device.

```python
import math
import jax
import jax.numpy as jnp
from jax import lax

MEMBERS = 64
VARS = 6
BINS = 256
NLAT = 96
LON = 352


def plant(result, rng, low, largest):
    place = [jax.random.randint(jax.random.fold_in(rng, axis), (), 0, length) for axis, length in enumerate(result.shape)]
    widest = result.shape.index(max(result.shape))
    beside = place[:widest] + [(place[widest] + 1) % result.shape[widest]] + place[widest + 1:]
    return result.at[tuple(place)].set(low).at[tuple(beside)].set(largest)


def setup_inputs(seed: int = 0) -> dict:
    streams_of = jax.random.split(jax.random.key(seed), 5)
    codes = plant(jax.random.randint(streams_of[0], (MEMBERS, NLAT, VARS, LON), -127, 128), jax.random.fold_in(streams_of[0], 1), -127, 127).astype(jnp.int32)
    exponents = plant(jax.random.randint(streams_of[1], (MEMBERS, NLAT, VARS), -8, -3), jax.random.fold_in(streams_of[1], 1), -8, (-3) - 1).astype(jnp.int32)
    centers = jnp.clip(jax.random.uniform(streams_of[2], (VARS, BINS), jnp.float32, -3.0, 3.0), -3.0, 3.0)
    widths = jnp.clip(jnp.exp(jax.random.uniform(streams_of[3], (VARS,), jnp.float32, math.log(0.01), math.log(0.03))), 0.01, 0.03)
    return dict(codes=codes, exponents=exponents, centers=centers, widths=widths)


def var_density(item, center, width):
    field = item.astype(jnp.float32)
    scaled = (center[None, None, None, :] - field[:, :, :, None]) / width
    total = lax.optimization_barrier(jnp.sum(jnp.exp(-0.5 * scaled * scaled), axis=0))
    return total / (field.shape[0] * width * math.sqrt(2.0 * math.pi))

def block_density(values, centers, widths):
    items = jnp.transpose(values, (2, 0, 1, 3))
    dens = lax.map(lambda t: var_density(t[0], t[1], t[2]), (items, centers, widths))
    return jnp.transpose(dens, (1, 0, 2, 3)).astype(jnp.bfloat16)

def reference(codes, exponents, centers, widths):
    scale = jnp.exp2(exponents.astype(jnp.float32))
    values = (codes.astype(jnp.float32) * scale[..., None]).astype(jnp.bfloat16)
    dens = block_density(values, centers, widths).astype(jnp.float32)
    padded = jnp.pad(dens, ((2, 2), (0, 0), (2, 2), (0, 0)))
    lat_sum = padded[0:NLAT] + padded[1:NLAT + 1] + padded[2:NLAT + 2] + padded[3:NLAT + 3] + padded[4:NLAT + 4]
    total = lat_sum[:, :, 0:LON] + lat_sum[:, :, 1:LON + 1] + lat_sum[:, :, 2:LON + 2] + lat_sum[:, :, 3:LON + 3] + lat_sum[:, :, 4:LON + 4]
    return (total / 25.0).astype(jnp.bfloat16)
```

```python
import functools
import math

import jax
import jax.numpy as jnp
import numpy as np
from jax import lax
from jax.experimental import pallas as pl
from jax.experimental.pallas import tpu as pltpu
from jax.sharding import PartitionSpec as P

REACH = 2
FINE = 256.0
OUTSIDE = 16.0
HALF = 384
POINTS = 2 * HALF
FIELDS = 16
WORDS = POINTS // FIELDS
VMEM = 48 * 1024 * 1024


def regroup_kernel(n, cells, width, codes_ref, scale_ref, out_ref):
    members, rows, items, _ = codes_ref.shape
    wide = cells + 2 * REACH
    edge = jnp.full((members, REACH), OUTSIDE, jnp.float32)
    rest = jnp.full((members, width - rows * wide), OUTSIDE, jnp.float32)
    for v in range(items):
        lines = []
        for r in range(rows):
            line = codes_ref[:, r, v, :].astype(jnp.float32)
            line = line * scale_ref[v, :, r : r + 1]
            lines.append(jnp.concatenate([edge, line, edge], axis=1))
        for d in range(n):
            parts = [line[:, d * cells : d * cells + wide] for line in lines]
            out_ref[d, v] = jnp.concatenate(parts + [rest], axis=1).astype(jnp.bfloat16)


def density_kernel(vals_ref, centers_ref, widths_ref, out_ref, table, words, steps, counts, bytes4):
    item = pl.program_id(0)
    n, _, members, width = vals_ref.shape
    total = n * members
    bins = centers_ref.shape[1]
    wide = widths_ref[item]

    point = lax.broadcasted_iota(jnp.int32, (1, POINTS), 1)
    mag = jnp.where(point >= HALF, point - HALF, point)
    octave = jnp.maximum(mag - 64, 0) >> 6
    mag = jnp.where(mag < 128, mag, (mag - 64 * octave) << octave).astype(jnp.float32)
    value = jnp.where(point >= HALF, -mag, mag) * (1.0 / FINE)
    scaled = (centers_ref[0] - value) / wide
    table[...] = jnp.exp(-0.5 * scaled * scaled).astype(jnp.bfloat16)

    for i in range(n):
        vals = vals_ref[i, 0].astype(jnp.float32) * FINE
        size = jnp.abs(vals).astype(jnp.int32)
        octave = jnp.zeros_like(size)
        for limit in (128, 256, 512, 1024):
            octave = octave + jnp.where(size >= limit, 1, 0)
        index = (size >> octave) + 64 * octave + jnp.where(vals < 0, HALF, 0)
        field = (index * (65536 // WORDS + 1)) >> 16
        there = size < 2048
        words[i * members : (i + 1) * members] = jnp.where(there, index - WORDS * field, WORDS)
        steps[i * members : (i + 1) * members] = jnp.left_shift(1, jnp.where(there, 2 * field, 0))

    norm = 1.0 / (total * wide * math.sqrt(2.0 * math.pi))
    lanes = 128
    groups = width // lanes
    counts[...] = jnp.zeros_like(counts)

    def finish(g):
        dens = jnp.dot(table[...], counts[...], preferred_element_type=jnp.float32)
        out_ref[0, :, pl.ds(pl.multiple_of(g * lanes, lanes), lanes)] = (dens * norm).astype(jnp.bfloat16)

    def group(g, _):
        finish(jnp.maximum(g - 1, 0))
        at = pl.ds(pl.multiple_of(g * lanes, lanes), lanes)
        row = lax.broadcasted_iota(jnp.int32, (WORDS, lanes), 0)
        for start in range(0, total, 15):
            stop = min(start + 15, total)
            raw = odd = None
            for first in range(start, stop, 3):
                pair = None
                for m in range(first, min(first + 3, stop)):
                    one = jnp.where(row == words[m : m + 1, at], steps[m : m + 1, at], 0)
                    pair = one if pair is None else pair + one
                high = lax.shift_right_logical(pair, 2) & 0x33333333
                raw = pair if raw is None else raw + pair
                odd = high if odd is None else odd + high
            even = raw - (odd << 2)
            for k, four in enumerate((even, odd)):
                low = four & 0x0F0F0F0F
                high = lax.shift_right_logical(four, 4) & 0x0F0F0F0F
                if start == 0:
                    bytes4[k] = low
                    bytes4[k + 2] = high
                else:
                    bytes4[k] += low
                    bytes4[k + 2] += high
        for f in range(FIELDS):
            part = lax.shift_right_logical(bytes4[f % 4], 8 * (f // 4))
            if f // 4 < 3:
                part = part & 0xFF
            counts[f * WORDS : (f + 1) * WORDS] = part.astype(jnp.float32).astype(jnp.bfloat16)
        return 0

    lax.fori_loop(0, groups, group, 0)
    finish(groups - 1)


def window_kernel(rows, cells, own_ref, top_ref, bottom_ref, mix_ref, mix_top_ref, mix_bottom_ref, out_ref):
    edge = mix_top_ref.shape[0]
    dims = (((1,), (1,)), ((), ()))
    def mixed(mix, dens):
        return lax.dot_general(mix, dens, dims, preferred_element_type=jnp.float32)
    above = mixed(mix_top_ref[...], top_ref[0])
    below = mixed(mix_bottom_ref[...], bottom_ref[0])
    full = mixed(mix_ref[...], own_ref[0])
    for r in range(rows):
        part = full[r * cells : (r + 1) * cells]
        if r < REACH:
            part = part + above[r * cells : (r + 1) * cells]
        if r >= rows - REACH:
            at = edge - (rows - r) * cells
            part = part + below[at : at + cells]
        out_ref[r, 0] = (part / 25.0).astype(jnp.bfloat16)


def window(rows, first, cells, width, source, source_first):
    wide = cells + 2 * REACH
    out = np.arange(rows * cells)
    lane = np.arange(width)
    dr = np.abs((out // cells + first)[:, None] - (lane // wide + source_first)[None, :])
    dl = (lane % wide)[None, :] - (out % cells)[:, None]
    inside = (dr <= REACH) & (dl >= 0) & (dl <= 2 * REACH) & (lane < source * wide)[None, :]
    return jnp.asarray(inside, jnp.bfloat16)


def solution(mesh):
    n = mesh.shape["member"]
    count = mesh.shape["band"]

    def shards(codes, exponents, centers, widths):
        members, rows, items, lon = codes.shape
        bins = centers.shape[1]
        cells = lon // n
        wide = cells + 2 * REACH
        width = -(-rows * wide // 128) * 128
        scale = jnp.left_shift(1, exponents + 8).astype(jnp.float32) * (1.0 / FINE)
        scale = jnp.transpose(scale, (2, 0, 1))
        params = pltpu.CompilerParams(vmem_limit_bytes=VMEM)
        values = pl.pallas_call(
            functools.partial(regroup_kernel, n, cells, width),
            out_shape=jax.ShapeDtypeStruct((n, items, members, width), jnp.bfloat16),
            compiler_params=params,
        )(codes, scale)
        values = lax.all_to_all(values, "member", split_axis=0, concat_axis=0, tiled=True)
        dens = pl.pallas_call(
            density_kernel,
            grid=(items,),
            in_specs=[
                pl.BlockSpec((n, 1, members, width), lambda v: (0, v, 0, 0)),
                pl.BlockSpec((1, bins, 1), lambda v: (v, 0, 0)),
                pl.BlockSpec(memory_space=pltpu.SMEM),
            ],
            out_specs=pl.BlockSpec((1, bins, width), lambda v: (v, 0, 0)),
            out_shape=jax.ShapeDtypeStruct((items, bins, width), jnp.bfloat16),
            scratch_shapes=[
                pltpu.VMEM((bins, POINTS), jnp.bfloat16),
                pltpu.VMEM((n * members, width), jnp.int32),
                pltpu.VMEM((n * members, width), jnp.int32),
                pltpu.VMEM((POINTS, 128), jnp.bfloat16),
                pltpu.VMEM((4, WORDS, 128), jnp.int32),
            ],
            compiler_params=params,
        )(values, centers[:, :, None], widths)
        edge = REACH * wide
        head = dens[:, :, :edge]
        tail = dens[:, :, (rows - REACH) * wide : rows * wide]
        top = lax.ppermute(tail, "band", [(i, i + 1) for i in range(count - 1)])
        bottom = lax.ppermute(head, "band", [(i + 1, i) for i in range(count - 1)])
        mix = window(rows, 0, cells, width, rows, 0)
        mix_top = window(REACH, 0, cells, edge, REACH, -REACH)
        mix_bottom = window(REACH, rows - REACH, cells, edge, REACH, rows)
        whole = pl.BlockSpec(memory_space=pltpu.VMEM)
        return pl.pallas_call(
            functools.partial(window_kernel, rows, cells),
            grid=(items,),
            in_specs=[
                pl.BlockSpec((1, bins, width), lambda v: (v, 0, 0)),
                pl.BlockSpec((1, bins, edge), lambda v: (v, 0, 0)),
                pl.BlockSpec((1, bins, edge), lambda v: (v, 0, 0)),
                whole,
                whole,
                whole,
            ],
            out_specs=pl.BlockSpec((rows, 1, cells, bins), lambda v: (0, v, 0, 0)),
            out_shape=jax.ShapeDtypeStruct((rows, items, cells, bins), jnp.bfloat16),
            compiler_params=params,
        )(dens, top, bottom, mix, mix_top, mix_bottom)

    return jax.shard_map(
        shards,
        mesh=mesh,
        in_specs=(P("member", "band", None, None), P("member", "band", None), P(), P()),
        out_specs=P("band", None, "member", None),
        check_vma=False,
    )
```

```python
import functools
import math

import jax
import jax.numpy as jnp
import numpy as np
from jax import lax
from jax.experimental import pallas as pl
from jax.experimental.pallas import tpu as pltpu
from jax.sharding import PartitionSpec as P

MESH = pl.DeviceIdType.MESH
REACH = 2
FINE = 256.0
OUTSIDE = 16.0
HALF = 384
POINTS = 2 * HALF
FIELDS = 16
WORDS = POINTS // FIELDS
VMEM = 48 * 1024 * 1024


def regroup(codes_ref, scale_ref, v, n, cells, width):
    rows, _, members, _ = codes_ref.shape
    wide = cells + 2 * REACH
    edge = jnp.full((members, REACH), OUTSIDE, jnp.float32)
    rest = jnp.full((members, width - rows * wide), OUTSIDE, jnp.float32)
    lines = []
    for r in range(rows):
        line = codes_ref[r, v].astype(jnp.float32)
        line = line * scale_ref[v, :, r : r + 1]
        lines.append(jnp.concatenate([edge, line, edge], axis=1))
    for d in range(n):
        parts = [line[:, d * cells : d * cells + wide] for line in lines]
        yield d, jnp.concatenate(parts + [rest], axis=1).astype(jnp.bfloat16)


def density_kernel(
    n, count, cells, width, lead, trail,
    codes_ref, scale_ref, centers_ref, widths_ref,
    own_ref, top_ref, bottom_ref,
    send, recv, dens, zeros, table, words, steps, counts, bytes4,
    send_sem, recv_sem, up_sem, down_sem, own_sem, zero_sem,
):
    rows, items, members, _ = codes_ref.shape
    total = n * members
    bins = centers_ref.shape[1]
    lanes = 128
    groups = width // lanes
    me = lax.axis_index("member")
    band = lax.axis_index("band")

    barrier = pltpu.get_barrier_semaphore()
    for o in range(1, n):
        pl.semaphore_signal(barrier, inc=1, device_id=(lax.rem(me + o, n), band), device_id_type=MESH)

    @pl.when(band > 0)
    def _():
        pl.semaphore_signal(barrier, inc=1, device_id=(me, band - 1), device_id_type=MESH)

    @pl.when(band < count - 1)
    def _():
        pl.semaphore_signal(barrier, inc=1, device_id=(me, band + 1), device_id_type=MESH)

    def outgoing(v, o):
        return pltpu.make_async_remote_copy(
            src_ref=send.at[v, lax.rem(me + o, n)],
            dst_ref=recv.at[v, o - 1],
            send_sem=send_sem.at[v, o - 1],
            recv_sem=recv_sem.at[v, o - 1],
            device_id=(lax.rem(me + o, n), band),
            device_id_type=MESH,
        )

    def upward(v):
        return pltpu.make_async_remote_copy(
            src_ref=dens.at[v, :, pl.ds(width - trail, trail)],
            dst_ref=top_ref.at[v],
            send_sem=up_sem.at[v, 0],
            recv_sem=up_sem.at[v, 1],
            device_id=(me, band + 1),
            device_id_type=MESH,
        )

    def downward(v):
        return pltpu.make_async_remote_copy(
            src_ref=dens.at[v, :, pl.ds(0, lead)],
            dst_ref=bottom_ref.at[v],
            send_sem=down_sem.at[v, 0],
            recv_sem=down_sem.at[v, 1],
            device_id=(me, band - 1),
            device_id_type=MESH,
        )

    def blank(v, side):
        if side == 0:
            return pltpu.make_async_copy(zeros.at[:, pl.ds(0, trail)], top_ref.at[v], zero_sem.at[0, v])
        return pltpu.make_async_copy(zeros.at[:, pl.ds(0, lead)], bottom_ref.at[v], zero_sem.at[1, v])

    def keep(v):
        return pltpu.make_async_copy(dens.at[v], own_ref.at[v], own_sem.at[v])

    for v in range(items):
        for d, block in regroup(codes_ref, scale_ref, v, n, cells, width):
            send[v, d] = block
        if v == 0:
            beside = jnp.where(band > 0, 1, 0) + jnp.where(band < count - 1, 1, 0)
            pl.semaphore_wait(barrier, n - 1 + beside)
        for o in range(1, n):
            outgoing(v, o).start()

    zeros[...] = jnp.zeros_like(zeros)

    @pl.when(band == 0)
    def _():
        for v in range(items):
            blank(v, 0).start()

    @pl.when(band == count - 1)
    def _():
        for v in range(items):
            blank(v, 1).start()

    counts[...] = jnp.zeros_like(counts)

    def item(v, _):
        wide = widths_ref[v]
        point = lax.broadcasted_iota(jnp.int32, (1, POINTS), 1)
        mag = jnp.where(point >= HALF, point - HALF, point)
        octave = jnp.maximum(mag - 64, 0) >> 6
        mag = jnp.where(mag < 128, mag, (mag - 64 * octave) << octave).astype(jnp.float32)
        value = jnp.where(point >= HALF, -mag, mag) * (1.0 / FINE)
        cross = lax.broadcasted_iota(jnp.int32, (bins, bins), 0) == lax.broadcasted_iota(jnp.int32, (bins, bins), 1)
        center = jnp.sum(jnp.where(cross, centers_ref[pl.ds(v, 1), :], 0.0), axis=1, keepdims=True)
        scaled = (center - value) / wide
        table[...] = jnp.exp(-0.5 * scaled * scaled).astype(jnp.bfloat16)

        for i in range(n):
            if i == 0:
                vals = send[v, me]
            else:
                outgoing(v, i).wait_recv()
                vals = recv[v, i - 1]
            vals = vals.astype(jnp.float32) * FINE
            size = jnp.abs(vals).astype(jnp.int32)
            octave = jnp.zeros_like(size)
            for limit in (128, 256, 512, 1024):
                octave = octave + jnp.where(size >= limit, 1, 0)
            index = (size >> octave) + 64 * octave + jnp.where(vals < 0, HALF, 0)
            field = (index * (65536 // WORDS + 1)) >> 16
            there = size < 2048
            words[i * members : (i + 1) * members] = jnp.where(there, index - WORDS * field, WORDS)
            steps[i * members : (i + 1) * members] = jnp.left_shift(1, jnp.where(there, 2 * field, 0))

        norm = 1.0 / (total * wide * math.sqrt(2.0 * math.pi))

        def finish(g):
            part = jnp.dot(table[...], counts[...], preferred_element_type=jnp.float32)
            at = pl.ds(pl.multiple_of(g * lanes, lanes), lanes)
            dens[v, :, at] = (part * norm).astype(jnp.bfloat16)

        def group(g, _):
            finish(jnp.maximum(g - 1, 0))
            at = pl.ds(pl.multiple_of(g * lanes, lanes), lanes)
            row = lax.broadcasted_iota(jnp.int32, (WORDS, lanes), 0)
            for start in range(0, total, 15):
                stop = min(start + 15, total)
                raw = odd = None
                for first in range(start, stop, 3):
                    pair = None
                    for m in range(first, min(first + 3, stop)):
                        one = jnp.where(row == words[m : m + 1, at], steps[m : m + 1, at], 0)
                        pair = one if pair is None else pair + one
                    high = lax.shift_right_logical(pair, 2) & 0x33333333
                    raw = pair if raw is None else raw + pair
                    odd = high if odd is None else odd + high
                even = raw - (odd << 2)
                for k, four in enumerate((even, odd)):
                    low = four & 0x0F0F0F0F
                    high = lax.shift_right_logical(four, 4) & 0x0F0F0F0F
                    if start == 0:
                        bytes4[k] = low
                        bytes4[k + 2] = high
                    else:
                        bytes4[k] += low
                        bytes4[k + 2] += high
            for f in range(FIELDS):
                part = lax.shift_right_logical(bytes4[f % 4], 8 * (f // 4))
                if f // 4 < 3:
                    part = part & 0xFF
                counts[f * WORDS : (f + 1) * WORDS] = part.astype(jnp.float32).astype(jnp.bfloat16)
            return 0

        lax.fori_loop(0, groups, group, 0)
        finish(groups - 1)
        keep(v).start()

        @pl.when(band > 0)
        def _():
            downward(v).start()

        @pl.when(band < count - 1)
        def _():
            upward(v).start()

        return 0

    lax.fori_loop(0, items, item, 0)

    for v in range(items):
        keep(v).wait()
        for o in range(1, n):
            outgoing(v, o).wait_send()

    @pl.when(band > 0)
    def _():
        for v in range(items):
            downward(v).wait_send()
            upward(v).wait_recv()

    @pl.when(band < count - 1)
    def _():
        for v in range(items):
            upward(v).wait_send()
            downward(v).wait_recv()

    @pl.when(band == 0)
    def _():
        for v in range(items):
            blank(v, 0).wait()

    @pl.when(band == count - 1)
    def _():
        for v in range(items):
            blank(v, 1).wait()


def window_kernel(rows, cells, own_ref, top_ref, bottom_ref, mix_ref, mix_top_ref, mix_bottom_ref, out_ref):
    edge = mix_top_ref.shape[0]
    dims = (((1,), (1,)), ((), ()))
    def mixed(mix, dens):
        return lax.dot_general(mix, dens, dims, preferred_element_type=jnp.float32)
    above = mixed(mix_top_ref[...], top_ref[0])
    below = mixed(mix_bottom_ref[...], bottom_ref[0])
    full = mixed(mix_ref[...], own_ref[0])
    for r in range(rows):
        part = full[r * cells : (r + 1) * cells]
        if r < REACH:
            part = part + above[r * cells : (r + 1) * cells]
        if r >= rows - REACH:
            at = edge - (rows - r) * cells
            part = part + below[at : at + cells]
        out_ref[r, 0] = (part / 25.0).astype(jnp.bfloat16)


def window(rows, first, cells, lanes, source_rows, source_first):
    wide = cells + 2 * REACH
    out = np.arange(rows * cells)
    row, place = lanes // wide, lanes % wide
    dr = np.abs((out // cells + first)[:, None] - (row + source_first)[None, :])
    dl = place[None, :] - (out % cells)[:, None]
    real = (row >= source_rows[0]) & (row < source_rows[1])
    inside = (dr <= REACH) & (dl >= 0) & (dl <= 2 * REACH) & real[None, :]
    return jnp.asarray(inside, jnp.bfloat16)


def solution(mesh):
    n = mesh.shape["member"]
    count = mesh.shape["band"]

    def shards(codes, exponents, centers, widths):
        members, rows, items, lon = codes.shape
        bins = centers.shape[1]
        cells = lon // n
        wide = cells + 2 * REACH
        width = -(-rows * wide // 128) * 128
        scale = jnp.left_shift(1, exponents + 8).astype(jnp.float32) * (1.0 / FINE)
        scale = jnp.transpose(scale, (2, 0, 1))
        codes = jnp.transpose(codes, (1, 2, 0, 3))
        lead = -(-REACH * wide // 128) * 128
        trail = width - (rows - REACH) * wide // 128 * 128
        params = pltpu.CompilerParams(vmem_limit_bytes=VMEM)
        vmem = pl.BlockSpec(memory_space=pltpu.VMEM)
        hbm = pl.BlockSpec(memory_space=pl.ANY)
        dens, top, bottom = pl.pallas_call(
            functools.partial(density_kernel, n, count, cells, width, lead, trail),
            in_specs=[vmem, vmem, vmem, pl.BlockSpec(memory_space=pltpu.SMEM)],
            out_specs=[hbm, hbm, hbm],
            out_shape=[
                jax.ShapeDtypeStruct((items, bins, width), jnp.bfloat16),
                jax.ShapeDtypeStruct((items, bins, trail), jnp.bfloat16),
                jax.ShapeDtypeStruct((items, bins, lead), jnp.bfloat16),
            ],
            scratch_shapes=[
                pltpu.VMEM((items, n, members, width), jnp.bfloat16),
                pltpu.VMEM((items, max(n - 1, 1), members, width), jnp.bfloat16),
                pltpu.VMEM((items, bins, width), jnp.bfloat16),
                pltpu.VMEM((bins, max(lead, trail)), jnp.bfloat16),
                pltpu.VMEM((bins, POINTS), jnp.bfloat16),
                pltpu.VMEM((n * members, width), jnp.int32),
                pltpu.VMEM((n * members, width), jnp.int32),
                pltpu.VMEM((POINTS, 128), jnp.bfloat16),
                pltpu.VMEM((4, WORDS, 128), jnp.int32),
                pltpu.SemaphoreType.DMA((items, n)),
                pltpu.SemaphoreType.DMA((items, n)),
                pltpu.SemaphoreType.DMA((items, 2)),
                pltpu.SemaphoreType.DMA((items, 2)),
                pltpu.SemaphoreType.DMA((items,)),
                pltpu.SemaphoreType.DMA((2, items)),
            ],
            compiler_params=pltpu.CompilerParams(
                vmem_limit_bytes=VMEM, collective_id=0, has_side_effects=True
            ),
        )(codes, scale, centers, widths)
        mix = window(rows, 0, cells, np.arange(width), (0, rows), 0)
        mix_top = window(REACH, 0, cells, np.arange(width - trail, width), (rows - REACH, rows), -rows)
        mix_bottom = window(REACH, rows - REACH, cells, np.arange(lead), (0, REACH), rows)
        whole = pl.BlockSpec(memory_space=pltpu.VMEM)
        return pl.pallas_call(
            functools.partial(window_kernel, rows, cells),
            grid=(items,),
            in_specs=[
                pl.BlockSpec((1, bins, width), lambda v: (v, 0, 0)),
                pl.BlockSpec((1, bins, trail), lambda v: (v, 0, 0)),
                pl.BlockSpec((1, bins, lead), lambda v: (v, 0, 0)),
                whole,
                whole,
                whole,
            ],
            out_specs=pl.BlockSpec((rows, 1, cells, bins), lambda v: (0, v, 0, 0)),
            out_shape=jax.ShapeDtypeStruct((rows, items, cells, bins), jnp.bfloat16),
            compiler_params=params,
        )(dens, top, bottom, mix, mix_top, mix_bottom)

    return jax.shard_map(
        shards,
        mesh=mesh,
        in_specs=(P("member", "band", None, None), P("member", "band", None), P(), P()),
        out_specs=P("band", None, "member", None),
        check_vma=False,
    )
```

```python
import functools
import math

import jax
import jax.numpy as jnp
import numpy as np
from jax import lax
from jax.experimental import pallas as pl
from jax.experimental.pallas import tpu as pltpu
from jax.sharding import PartitionSpec as P

MESH = pl.DeviceIdType.MESH
REACH = 2
FINE = 256.0
OUTSIDE = 16.0
HALF = 384
POINTS = 2 * HALF
FIELDS = 16
WORDS = POINTS // FIELDS
VMEM = 60 * 1024 * 1024
AHEAD = 2


def regroup(codes_ref, exponents_ref, v, n, cells, width):
    rows, _, members, _ = codes_ref.shape
    wide = cells + 2 * REACH
    lon = codes_ref.shape[3]
    edge = jnp.full((members, REACH), OUTSIDE, jnp.float32)
    rest = jnp.full((members, width - rows * wide), OUTSIDE, jnp.float32)
    scale = jnp.left_shift(1, exponents_ref[v] + 8).astype(jnp.float32) * (1.0 / FINE)
    lines = [codes_ref[r, v].astype(jnp.float32) * scale[:, r : r + 1] for r in range(rows)]
    for d in range(n):
        low, high = d * cells - REACH, (d + 1) * cells + REACH
        parts = []
        for line in lines:
            if low < 0:
                parts.append(edge)
            parts.append(line[:, max(low, 0) : min(high, lon)])
            if high > lon:
                parts.append(edge)
        yield d, jnp.concatenate(parts + [rest], axis=1).astype(jnp.bfloat16)


def density_kernel(
    n, count, cells, width, lead, trail,
    codes_ref, exponents_ref, centers_ref, widths_ref,
    own_ref, top_ref, bottom_ref,
    send, recv, dens, zeros, table, words, steps, counts, bytes4,
    send_sem, recv_sem, up_sem, down_sem, own_sem, zero_sem,
):
    rows, items, members, _ = codes_ref.shape
    total = n * members
    bins = centers_ref.shape[1]
    lanes = 128
    groups = width // lanes
    me = lax.axis_index("member")
    band = lax.axis_index("band")

    barrier = pltpu.get_barrier_semaphore()
    for o in range(1, n):
        pl.semaphore_signal(barrier, inc=1, device_id=(lax.rem(me + o, n), band), device_id_type=MESH)

    @pl.when(band > 0)
    def _():
        pl.semaphore_signal(barrier, inc=1, device_id=(me, band - 1), device_id_type=MESH)

    @pl.when(band < count - 1)
    def _():
        pl.semaphore_signal(barrier, inc=1, device_id=(me, band + 1), device_id_type=MESH)

    def outgoing(v, o):
        return pltpu.make_async_remote_copy(
            src_ref=send.at[v, lax.rem(me + o, n)],
            dst_ref=recv.at[v, o - 1],
            send_sem=send_sem.at[v, o - 1],
            recv_sem=recv_sem.at[v, o - 1],
            device_id=(lax.rem(me + o, n), band),
            device_id_type=MESH,
        )

    def upward(v):
        return pltpu.make_async_remote_copy(
            src_ref=dens.at[v, :, pl.ds(width - trail, trail)],
            dst_ref=top_ref.at[v],
            send_sem=up_sem.at[v, 0],
            recv_sem=up_sem.at[v, 1],
            device_id=(me, band + 1),
            device_id_type=MESH,
        )

    def downward(v):
        return pltpu.make_async_remote_copy(
            src_ref=dens.at[v, :, pl.ds(0, lead)],
            dst_ref=bottom_ref.at[v],
            send_sem=down_sem.at[v, 0],
            recv_sem=down_sem.at[v, 1],
            device_id=(me, band - 1),
            device_id_type=MESH,
        )

    def blank(v, side):
        if side == 0:
            return pltpu.make_async_copy(zeros.at[:, pl.ds(0, trail)], top_ref.at[v], zero_sem.at[0, v])
        return pltpu.make_async_copy(zeros.at[:, pl.ds(0, lead)], bottom_ref.at[v], zero_sem.at[1, v])

    def keep(v):
        return pltpu.make_async_copy(dens.at[v], own_ref.at[v], own_sem.at[v])

    for v in range(items):
        for d, block in regroup(codes_ref, exponents_ref, v, n, cells, width):
            send[v, d] = block
        if v == 0:
            beside = jnp.where(band > 0, 1, 0) + jnp.where(band < count - 1, 1, 0)
            pl.semaphore_wait(barrier, n - 1 + beside)
        if v < AHEAD:
            for o in range(1, n):
                outgoing(v, o).start()

    zeros[...] = jnp.zeros_like(zeros)

    @pl.when(band == 0)
    def _():
        for v in range(items):
            blank(v, 0).start()

    @pl.when(band == count - 1)
    def _():
        for v in range(items):
            blank(v, 1).start()

    counts[...] = jnp.zeros_like(counts)

    def item(v, _):
        wide = widths_ref[v]
        point = lax.broadcasted_iota(jnp.int32, (1, POINTS), 1)
        mag = jnp.where(point >= HALF, point - HALF, point)
        octave = jnp.maximum(mag - 64, 0) >> 6
        mag = jnp.where(mag < 128, mag, (mag - 64 * octave) << octave).astype(jnp.float32)
        value = jnp.where(point >= HALF, -mag, mag) * (1.0 / FINE)
        cross = lax.broadcasted_iota(jnp.int32, (bins, bins), 0) == lax.broadcasted_iota(jnp.int32, (bins, bins), 1)
        center = jnp.sum(jnp.where(cross, centers_ref[pl.ds(v, 1), :], 0.0), axis=1, keepdims=True)
        scaled = (center - value) / wide
        norm = 1.0 / (total * wide * math.sqrt(2.0 * math.pi))
        table[...] = (jnp.exp(-0.5 * scaled * scaled) * norm).astype(jnp.bfloat16)

        for o in range(1, n):
            outgoing(v, o).wait_recv()

        @pl.when(v + AHEAD < items)
        def _():
            for o in range(1, n):
                outgoing(v + AHEAD, o).start()


        for i in range(n):
            if i == 0:
                vals = send[v, me]
            else:
                vals = recv[v, i - 1]
            vals = vals.astype(jnp.float32) * FINE
            size = jnp.abs(vals).astype(jnp.int32)
            octave = jnp.zeros_like(size)
            for limit in (128, 256, 512, 1024):
                octave = octave + jnp.where(size >= limit, 1, 0)
            index = (size >> octave) + 64 * octave + jnp.where(vals < 0, HALF, 0)
            field = (index * (65536 // WORDS + 1)) >> 16
            there = size < 2048
            words[i * members : (i + 1) * members] = jnp.where(there, index - WORDS * field, WORDS)
            steps[i * members : (i + 1) * members] = jnp.left_shift(1, jnp.where(there, 2 * field, 0))

        def finish(g):
            part = jnp.dot(table[...], counts[...], preferred_element_type=jnp.float32)
            at = pl.ds(pl.multiple_of(g * lanes, lanes), lanes)
            dens[v, :, at] = part.astype(jnp.bfloat16)

        def group(g, _):
            finish(jnp.maximum(g - 1, 0))
            at = pl.ds(pl.multiple_of(g * lanes, lanes), lanes)
            row = lax.broadcasted_iota(jnp.int32, (WORDS, lanes), 0)
            for start in range(0, total, 15):
                stop = min(start + 15, total)
                raw = odd = None
                for first in range(start, stop, 3):
                    pair = None
                    for m in range(first, min(first + 3, stop)):
                        one = jnp.where(row == words[m : m + 1, at], steps[m : m + 1, at], 0)
                        pair = one if pair is None else pair + one
                    high = lax.shift_right_logical(pair, 2) & 0x33333333
                    raw = pair if raw is None else raw + pair
                    odd = high if odd is None else odd + high
                even = raw - (odd << 2)
                for k, four in enumerate((even, odd)):
                    low = four & 0x0F0F0F0F
                    high = lax.shift_right_logical(four, 4) & 0x0F0F0F0F
                    if start == 0:
                        bytes4[k] = low
                        bytes4[k + 2] = high
                    else:
                        bytes4[k] += low
                        bytes4[k + 2] += high
            for f in range(FIELDS):
                part = lax.shift_right_logical(bytes4[f % 4], 8 * (f // 4))
                if f // 4 < 3:
                    part = part & 0xFF
                counts[f * WORDS : (f + 1) * WORDS] = part.astype(jnp.float32).astype(jnp.bfloat16)
            return 0

        lax.fori_loop(0, groups, group, 0)
        finish(groups - 1)
        keep(v).start()

        @pl.when(band > 0)
        def _():
            downward(v).start()

        @pl.when(band < count - 1)
        def _():
            upward(v).start()

        return 0

    lax.fori_loop(0, items, item, 0)

    for v in range(items):
        keep(v).wait()
        for o in range(1, n):
            outgoing(v, o).wait_send()

    @pl.when(band > 0)
    def _():
        for v in range(items):
            downward(v).wait_send()
            upward(v).wait_recv()

    @pl.when(band < count - 1)
    def _():
        for v in range(items):
            upward(v).wait_send()
            downward(v).wait_recv()

    @pl.when(band == 0)
    def _():
        for v in range(items):
            blank(v, 0).wait()

    @pl.when(band == count - 1)
    def _():
        for v in range(items):
            blank(v, 1).wait()


def window_kernel(rows, cells, chunks, own_ref, top_ref, bottom_ref, mix_ref, mix_top_ref, mix_bottom_ref, out_ref):
    edge = mix_top_ref.shape[0]
    dims = (((1,), (1,)), ((), ()))
    def mixed(mix, dens):
        return lax.dot_general(mix, dens, dims, preferred_element_type=jnp.float32)
    above = mixed(mix_top_ref[...], top_ref[0])
    below = mixed(mix_bottom_ref[...], bottom_ref[0])
    for c, (first, low, high) in enumerate(chunks):
        size = mix_ref.shape[1] // cells
        full = mixed(mix_ref[c, :, : high - low], own_ref[0, :, low:high])
        for r in range(first, first + size):
            part = full[(r - first) * cells : (r - first + 1) * cells]
            if r < REACH:
                part = part + above[r * cells : (r + 1) * cells]
            if r >= rows - REACH:
                at = edge - (rows - r) * cells
                part = part + below[at : at + cells]
            out_ref[r, 0] = (part / 25.0).astype(jnp.bfloat16)


def window(rows, first, cells, lanes, source_rows, source_first):
    wide = cells + 2 * REACH
    out = np.arange(rows * cells)
    row, place = lanes // wide, lanes % wide
    dr = np.abs((out // cells + first)[:, None] - (row + source_first)[None, :])
    dl = place[None, :] - (out % cells)[:, None]
    real = (row >= source_rows[0]) & (row < source_rows[1])
    inside = (dr <= REACH) & (dl >= 0) & (dl <= 2 * REACH) & real[None, :]
    return inside.astype(jnp.bfloat16)


def solution(mesh):
    n = mesh.shape["member"]
    count = mesh.shape["band"]

    def shards(codes, exponents, centers, widths):
        members, rows, items, lon = codes.shape
        bins = centers.shape[1]
        cells = lon // n
        wide = cells + 2 * REACH
        width = -(-rows * wide // 128) * 128
        exponents = jnp.transpose(exponents, (2, 0, 1))
        codes = jnp.transpose(codes, (1, 2, 0, 3))
        lead = -(-REACH * wide // 128) * 128
        trail = width - (rows - REACH) * wide // 128 * 128
        params = pltpu.CompilerParams(vmem_limit_bytes=VMEM)
        vmem = pl.BlockSpec(memory_space=pltpu.VMEM)
        hbm = pl.BlockSpec(memory_space=pl.ANY)
        dens, top, bottom = pl.pallas_call(
            functools.partial(density_kernel, n, count, cells, width, lead, trail),
            in_specs=[vmem, vmem, vmem, pl.BlockSpec(memory_space=pltpu.SMEM)],
            out_specs=[hbm, hbm, hbm],
            out_shape=[
                jax.ShapeDtypeStruct((items, bins, width), jnp.bfloat16),
                jax.ShapeDtypeStruct((items, bins, trail), jnp.bfloat16),
                jax.ShapeDtypeStruct((items, bins, lead), jnp.bfloat16),
            ],
            scratch_shapes=[
                pltpu.VMEM((items, n, members, width), jnp.bfloat16),
                pltpu.VMEM((items, max(n - 1, 1), members, width), jnp.bfloat16),
                pltpu.VMEM((items, bins, width), jnp.bfloat16),
                pltpu.VMEM((bins, max(lead, trail)), jnp.bfloat16),
                pltpu.VMEM((bins, POINTS), jnp.bfloat16),
                pltpu.VMEM((n * members, width), jnp.int32),
                pltpu.VMEM((n * members, width), jnp.int32),
                pltpu.VMEM((POINTS, 128), jnp.bfloat16),
                pltpu.VMEM((4, WORDS, 128), jnp.int32),
                pltpu.SemaphoreType.DMA((items, n)),
                pltpu.SemaphoreType.DMA((items, n)),
                pltpu.SemaphoreType.DMA((items, 2)),
                pltpu.SemaphoreType.DMA((items, 2)),
                pltpu.SemaphoreType.DMA((items,)),
                pltpu.SemaphoreType.DMA((2, items)),
            ],
            compiler_params=pltpu.CompilerParams(
                vmem_limit_bytes=VMEM, collective_id=0, has_side_effects=True
            ),
        )(codes, exponents, centers, widths)
        size = max(k for k in (3, 2, 1) if rows % k == 0)
        chunks = []
        for first in range(0, rows, size):
            low = max(first - REACH, 0) * wide // 128 * 128
            high = -(-min(first + size + REACH, rows) * wide // 128) * 128
            chunks.append((first, low, high))
        depth = max(high - low for _, low, high in chunks)
        mix = np.stack(
            [window(size, first, cells, np.arange(low, low + depth), (0, rows), 0) for first, low, _ in chunks]
        )
        mix_top = window(REACH, 0, cells, np.arange(width - trail, width), (rows - REACH, rows), -rows)
        mix_bottom = window(REACH, rows - REACH, cells, np.arange(lead), (0, REACH), rows)
        whole = pl.BlockSpec(memory_space=pltpu.VMEM)
        return pl.pallas_call(
            functools.partial(window_kernel, rows, cells, chunks),
            grid=(items,),
            in_specs=[
                pl.BlockSpec((1, bins, width), lambda v: (v, 0, 0)),
                pl.BlockSpec((1, bins, trail), lambda v: (v, 0, 0)),
                pl.BlockSpec((1, bins, lead), lambda v: (v, 0, 0)),
                whole,
                whole,
                whole,
            ],
            out_specs=pl.BlockSpec((rows, 1, cells, bins), lambda v: (0, v, 0, 0)),
            out_shape=jax.ShapeDtypeStruct((rows, items, cells, bins), jnp.bfloat16),
            compiler_params=params,
        )(dens, top, bottom, mix, mix_top, mix_bottom)

    return jax.shard_map(
        shards,
        mesh=mesh,
        in_specs=(P("member", "band", None, None), P("member", "band", None), P(), P()),
        out_specs=P("band", None, "member", None),
        check_vma=False,
    )
```

```python
import functools
import math

import jax
import jax.numpy as jnp
import numpy as np
from jax import lax
from jax.experimental import pallas as pl
from jax.experimental.pallas import tpu as pltpu
from jax.sharding import PartitionSpec as P

MESH = pl.DeviceIdType.MESH
REACH = 2
FINE = 256.0
OUTSIDE = 16.0
HALF = 384
POINTS = 2 * HALF
FIELDS = 16
WORDS = POINTS // FIELDS
VMEM = 60 * 1024 * 1024
AHEAD = 2


def regroup(codes_ref, exponents_ref, v, n, cells, width):
    rows, _, members, _ = codes_ref.shape
    wide = cells + 2 * REACH
    lon = codes_ref.shape[3]
    edge = jnp.full((members, REACH), OUTSIDE, jnp.float32)
    rest = jnp.full((members, width - rows * wide), OUTSIDE, jnp.float32)
    scale = jnp.left_shift(1, exponents_ref[v] + 8).astype(jnp.float32) * (1.0 / FINE)
    lines = [codes_ref[r, v].astype(jnp.float32) * scale[:, r : r + 1] for r in range(rows)]
    for d in range(n):
        low, high = d * cells - REACH, (d + 1) * cells + REACH
        parts = []
        for line in lines:
            if low < 0:
                parts.append(edge)
            parts.append(line[:, max(low, 0) : min(high, lon)])
            if high > lon:
                parts.append(edge)
        yield d, jnp.concatenate(parts + [rest], axis=1).astype(jnp.bfloat16)


def density_kernel(
    n, count, cells, width, lead, after, trail,
    codes_ref, exponents_ref, centers_ref, widths_ref,
    own_ref, top_ref, bottom_ref,
    send, recv, dens, zeros, table, words, steps, counts, bytes4,
    send_sem, recv_sem, up_sem, down_sem, own_sem, zero_sem,
):
    rows, items, members, _ = codes_ref.shape
    total = n * members
    bins = centers_ref.shape[1]
    lanes = 128
    groups = width // lanes
    front = -(-lead // lanes)
    back = min(groups - after // lanes, groups - front)
    me = lax.axis_index("member")
    band = lax.axis_index("band")

    barrier = pltpu.get_barrier_semaphore()
    for o in range(1, n):
        pl.semaphore_signal(barrier, inc=1, device_id=(lax.rem(me + o, n), band), device_id_type=MESH)

    @pl.when(band > 0)
    def _():
        pl.semaphore_signal(barrier, inc=1, device_id=(me, band - 1), device_id_type=MESH)

    @pl.when(band < count - 1)
    def _():
        pl.semaphore_signal(barrier, inc=1, device_id=(me, band + 1), device_id_type=MESH)

    def outgoing(v, o):
        return pltpu.make_async_remote_copy(
            src_ref=send.at[v, lax.rem(me + o, n)],
            dst_ref=recv.at[v, o - 1],
            send_sem=send_sem.at[v, o - 1],
            recv_sem=recv_sem.at[v, o - 1],
            device_id=(lax.rem(me + o, n), band),
            device_id_type=MESH,
        )

    def upward(v):
        return pltpu.make_async_remote_copy(
            src_ref=dens.at[v, pl.ds(after, trail)],
            dst_ref=top_ref.at[v],
            send_sem=up_sem.at[v, 0],
            recv_sem=up_sem.at[v, 1],
            device_id=(me, band + 1),
            device_id_type=MESH,
        )

    def downward(v):
        return pltpu.make_async_remote_copy(
            src_ref=dens.at[v, pl.ds(0, lead)],
            dst_ref=bottom_ref.at[v],
            send_sem=down_sem.at[v, 0],
            recv_sem=down_sem.at[v, 1],
            device_id=(me, band - 1),
            device_id_type=MESH,
        )

    def blank(v, side):
        if side == 0:
            return pltpu.make_async_copy(zeros.at[pl.ds(0, trail)], top_ref.at[v], zero_sem.at[0, v])
        return pltpu.make_async_copy(zeros.at[pl.ds(0, lead)], bottom_ref.at[v], zero_sem.at[1, v])

    def keep(v):
        return pltpu.make_async_copy(dens.at[v], own_ref.at[v], own_sem.at[v])

    for v in range(items):
        for d, block in regroup(codes_ref, exponents_ref, v, n, cells, width):
            send[v, d] = block
        if v == 0:
            beside = jnp.where(band > 0, 1, 0) + jnp.where(band < count - 1, 1, 0)
            pl.semaphore_wait(barrier, n - 1 + beside)
        if v < AHEAD:
            for o in range(1, n):
                outgoing(v, o).start()

    zeros[...] = jnp.zeros_like(zeros)

    @pl.when(band == 0)
    def _():
        for v in range(items):
            blank(v, 0).start()

    @pl.when(band == count - 1)
    def _():
        for v in range(items):
            blank(v, 1).start()

    counts[...] = jnp.zeros_like(counts)

    def item(v, _):
        wide = widths_ref[v]
        point = lax.broadcasted_iota(jnp.int32, (1, POINTS), 1)
        mag = jnp.where(point >= HALF, point - HALF, point)
        octave = jnp.maximum(mag - 64, 0) >> 6
        mag = jnp.where(mag < 128, mag, (mag - 64 * octave) << octave).astype(jnp.float32)
        value = jnp.where(point >= HALF, -mag, mag) * (1.0 / FINE)
        cross = lax.broadcasted_iota(jnp.int32, (bins, bins), 0) == lax.broadcasted_iota(jnp.int32, (bins, bins), 1)
        center = jnp.sum(jnp.where(cross, centers_ref[pl.ds(v, 1), :], 0.0), axis=1, keepdims=True)
        scaled = (center - value) / wide
        norm = 1.0 / (total * wide * math.sqrt(2.0 * math.pi))
        table[...] = (jnp.exp(-0.5 * scaled * scaled) * norm).astype(jnp.bfloat16)

        for o in range(1, n):
            outgoing(v, o).wait_recv()

        @pl.when(v + AHEAD < items)
        def _():
            for o in range(1, n):
                outgoing(v + AHEAD, o).start()


        for i in range(n):
            if i == 0:
                vals = send[v, me]
            else:
                vals = recv[v, i - 1]
            vals = vals.astype(jnp.float32) * FINE
            size = jnp.abs(vals).astype(jnp.int32)
            octave = jnp.zeros_like(size)
            for limit in (128, 256, 512, 1024):
                octave = octave + jnp.where(size >= limit, 1, 0)
            index = (size >> octave) + 64 * octave + jnp.where(vals < 0, HALF, 0)
            field = (index * (65536 // WORDS + 1)) >> 16
            there = size < 2048
            words[i * members : (i + 1) * members] = jnp.where(there, index - WORDS * field, WORDS)
            steps[i * members : (i + 1) * members] = jnp.left_shift(1, jnp.where(there, 2 * field, 0))

        def finish(g):
            part = jnp.dot(table[...], counts[...], preferred_element_type=jnp.float32)
            at = pl.ds(pl.multiple_of(g * lanes, lanes), lanes)
            dens[v, at] = jnp.transpose(part).astype(jnp.bfloat16)

        def place(i):
            spot = jnp.where(i < front + back, groups - back + i - front, i - back)
            return jnp.where(i < front, i, spot)

        def group(i, _, first):
            finish(place(jnp.maximum(i - 1, first)))
            g = place(i)
            at = pl.ds(pl.multiple_of(g * lanes, lanes), lanes)
            row = lax.broadcasted_iota(jnp.int32, (WORDS, lanes), 0)
            for start in range(0, total, 15):
                stop = min(start + 15, total)
                raw = odd = None
                for first in range(start, stop, 3):
                    pair = None
                    for m in range(first, min(first + 3, stop)):
                        one = jnp.where(row == words[m : m + 1, at], steps[m : m + 1, at], 0)
                        pair = one if pair is None else pair + one
                    high = lax.shift_right_logical(pair, 2) & 0x33333333
                    raw = pair if raw is None else raw + pair
                    odd = high if odd is None else odd + high
                even = raw - (odd << 2)
                for k, four in enumerate((even, odd)):
                    low = four & 0x0F0F0F0F
                    high = lax.shift_right_logical(four, 4) & 0x0F0F0F0F
                    if start == 0:
                        bytes4[k] = low
                        bytes4[k + 2] = high
                    else:
                        bytes4[k] += low
                        bytes4[k + 2] += high
            for f in range(FIELDS):
                part = lax.shift_right_logical(bytes4[f % 4], 8 * (f // 4))
                if f // 4 < 3:
                    part = part & 0xFF
                counts[f * WORDS : (f + 1) * WORDS] = part.astype(jnp.float32).astype(jnp.bfloat16)
            return 0

        lax.fori_loop(0, front + back, functools.partial(group, first=0), 0)
        finish(place(front + back - 1))

        @pl.when(band > 0)
        def _():
            downward(v).start()

        @pl.when(band < count - 1)
        def _():
            upward(v).start()

        if front + back < groups:
            lax.fori_loop(front + back, groups, functools.partial(group, first=front + back), 0)
            finish(place(groups - 1))
        keep(v).start()
        return 0

    lax.fori_loop(0, items, item, 0)

    for v in range(items):
        keep(v).wait()
        for o in range(1, n):
            outgoing(v, o).wait_send()

    @pl.when(band > 0)
    def _():
        for v in range(items):
            downward(v).wait_send()
            upward(v).wait_recv()

    @pl.when(band < count - 1)
    def _():
        for v in range(items):
            upward(v).wait_send()
            downward(v).wait_recv()

    @pl.when(band == 0)
    def _():
        for v in range(items):
            blank(v, 0).wait()

    @pl.when(band == count - 1)
    def _():
        for v in range(items):
            blank(v, 1).wait()


def window_kernel(rows, cells, chunks, own_ref, top_ref, bottom_ref, mix_ref, mix_top_ref, mix_bottom_ref, out_ref):
    edge = mix_top_ref.shape[0]
    dims = (((1,), (0,)), ((), ()))
    def mixed(mix, dens):
        return lax.dot_general(mix, dens, dims, preferred_element_type=jnp.float32)
    above = mixed(mix_top_ref[...], top_ref[0])
    below = mixed(mix_bottom_ref[...], bottom_ref[0])
    for c, (first, low, high) in enumerate(chunks):
        size = mix_ref.shape[1] // cells
        full = mixed(mix_ref[c, :, : high - low], own_ref[0, low:high])
        for r in range(first, first + size):
            part = full[(r - first) * cells : (r - first + 1) * cells]
            if r < REACH:
                part = part + above[r * cells : (r + 1) * cells]
            if r >= rows - REACH:
                at = edge - (rows - r) * cells
                part = part + below[at : at + cells]
            out_ref[r, 0] = (part * (1.0 / 25.0)).astype(jnp.bfloat16)


def window(rows, first, cells, lanes, source_rows, source_first):
    wide = cells + 2 * REACH
    out = np.arange(rows * cells)
    row, place = lanes // wide, lanes % wide
    dr = np.abs((out // cells + first)[:, None] - (row + source_first)[None, :])
    dl = place[None, :] - (out % cells)[:, None]
    real = (row >= source_rows[0]) & (row < source_rows[1])
    inside = (dr <= REACH) & (dl >= 0) & (dl <= 2 * REACH) & real[None, :]
    return inside.astype(jnp.bfloat16)


def solution(mesh):
    n = mesh.shape["member"]
    count = mesh.shape["band"]

    def shards(codes, exponents, centers, widths):
        members, rows, items, lon = codes.shape
        bins = centers.shape[1]
        cells = lon // n
        wide = cells + 2 * REACH
        width = -(-rows * wide // 128) * 128
        exponents = jnp.transpose(exponents, (2, 0, 1))
        codes = jnp.transpose(codes, (1, 2, 0, 3))
        lead = -(-REACH * wide // 16) * 16
        after = (rows - REACH) * wide // 16 * 16
        trail = -(-(rows * wide - after) // 16) * 16
        params = pltpu.CompilerParams(vmem_limit_bytes=VMEM)
        vmem = pl.BlockSpec(memory_space=pltpu.VMEM)
        hbm = pl.BlockSpec(memory_space=pl.ANY)
        dens, top, bottom = pl.pallas_call(
            functools.partial(density_kernel, n, count, cells, width, lead, after, trail),
            in_specs=[vmem, vmem, vmem, pl.BlockSpec(memory_space=pltpu.SMEM)],
            out_specs=[hbm, hbm, hbm],
            out_shape=[
                jax.ShapeDtypeStruct((items, width, bins), jnp.bfloat16),
                jax.ShapeDtypeStruct((items, trail, bins), jnp.bfloat16),
                jax.ShapeDtypeStruct((items, lead, bins), jnp.bfloat16),
            ],
            scratch_shapes=[
                pltpu.VMEM((items, n, members, width), jnp.bfloat16),
                pltpu.VMEM((items, max(n - 1, 1), members, width), jnp.bfloat16),
                pltpu.VMEM((items, width, bins), jnp.bfloat16),
                pltpu.VMEM((max(lead, trail), bins), jnp.bfloat16),
                pltpu.VMEM((bins, POINTS), jnp.bfloat16),
                pltpu.VMEM((n * members, width), jnp.int32),
                pltpu.VMEM((n * members, width), jnp.int32),
                pltpu.VMEM((POINTS, 128), jnp.bfloat16),
                pltpu.VMEM((4, WORDS, 128), jnp.int32),
                pltpu.SemaphoreType.DMA((items, n)),
                pltpu.SemaphoreType.DMA((items, n)),
                pltpu.SemaphoreType.DMA((items, 2)),
                pltpu.SemaphoreType.DMA((items, 2)),
                pltpu.SemaphoreType.DMA((items,)),
                pltpu.SemaphoreType.DMA((2, items)),
            ],
            compiler_params=pltpu.CompilerParams(
                vmem_limit_bytes=VMEM, collective_id=0, has_side_effects=True
            ),
        )(codes, exponents, centers, widths)
        size = max(k for k in (3, 2, 1) if rows % k == 0)
        chunks = []
        for first in range(0, rows, size):
            low = max(first - REACH, 0) * wide // 128 * 128
            high = -(-min(first + size + REACH, rows) * wide // 128) * 128
            chunks.append((first, low, high))
        depth = max(high - low for _, low, high in chunks)
        mix = np.stack(
            [window(size, first, cells, np.arange(low, low + depth), (0, rows), 0) for first, low, _ in chunks]
        )
        mix_top = window(REACH, 0, cells, np.arange(after, after + trail), (rows - REACH, rows), -rows)
        mix_bottom = window(REACH, rows - REACH, cells, np.arange(lead), (0, REACH), rows)
        whole = pl.BlockSpec(memory_space=pltpu.VMEM)
        return pl.pallas_call(
            functools.partial(window_kernel, rows, cells, chunks),
            grid=(items,),
            in_specs=[
                pl.BlockSpec((1, width, bins), lambda v: (v, 0, 0)),
                pl.BlockSpec((1, trail, bins), lambda v: (v, 0, 0)),
                pl.BlockSpec((1, lead, bins), lambda v: (v, 0, 0)),
                whole,
                whole,
                whole,
            ],
            out_specs=pl.BlockSpec((rows, 1, cells, bins), lambda v: (0, v, 0, 0)),
            out_shape=jax.ShapeDtypeStruct((rows, items, cells, bins), jnp.bfloat16),
            compiler_params=params,
        )(dens, top, bottom, mix, mix_top, mix_bottom)

    return jax.shard_map(
        shards,
        mesh=mesh,
        in_specs=(P("member", "band", None, None), P("member", "band", None), P(), P()),
        out_specs=P("band", None, "member", None),
        check_vma=False,
    )
```

```python
import functools
import math

import jax
import jax.numpy as jnp
import numpy as np
from jax import lax
from jax.experimental import pallas as pl
from jax.experimental.pallas import tpu as pltpu
from jax.sharding import PartitionSpec as P

MESH = pl.DeviceIdType.MESH
REACH = 2
FINE = 256.0
OUTSIDE = 16.0
HALF = 384
POINTS = 2 * HALF
FIELDS = 16
WORDS = POINTS // FIELDS
VMEM = 60 * 1024 * 1024
AHEAD = 2


def regroup(codes_ref, exponents_ref, v, n, cells, width):
    rows, _, members, _ = codes_ref.shape
    wide = cells + 2 * REACH
    lon = codes_ref.shape[3]
    edge = jnp.full((members, REACH), OUTSIDE, jnp.float32)
    rest = jnp.full((members, width - rows * wide), OUTSIDE, jnp.float32)
    scale = jnp.left_shift(1, exponents_ref[v] + 8).astype(jnp.float32) * (1.0 / FINE)
    lines = [codes_ref[r, v].astype(jnp.float32) * scale[:, r : r + 1] for r in range(rows)]
    for d in range(n):
        low, high = d * cells - REACH, (d + 1) * cells + REACH
        parts = []
        for line in lines:
            if low < 0:
                parts.append(edge)
            parts.append(line[:, max(low, 0) : min(high, lon)])
            if high > lon:
                parts.append(edge)
        yield d, jnp.concatenate(parts + [rest], axis=1).astype(jnp.bfloat16)


def density_kernel(
    n, count, cells, width, lead, trail,
    codes_ref, exponents_ref, centers_ref, widths_ref,
    own_ref, top_ref, bottom_ref,
    send, recv, dens, zeros, table, words, steps, counts, bytes4,
    send_sem, recv_sem, up_sem, down_sem, own_sem, zero_sem,
):
    rows, items, members, _ = codes_ref.shape
    total = n * members
    bins = centers_ref.shape[1]
    lanes = 128
    groups = width // lanes
    front = lead // lanes
    back = min(trail // lanes, groups - front)
    me = lax.axis_index("member")
    band = lax.axis_index("band")

    barrier = pltpu.get_barrier_semaphore()
    for o in range(1, n):
        pl.semaphore_signal(barrier, inc=1, device_id=(lax.rem(me + o, n), band), device_id_type=MESH)

    @pl.when(band > 0)
    def _():
        pl.semaphore_signal(barrier, inc=1, device_id=(me, band - 1), device_id_type=MESH)

    @pl.when(band < count - 1)
    def _():
        pl.semaphore_signal(barrier, inc=1, device_id=(me, band + 1), device_id_type=MESH)

    def outgoing(v, o):
        return pltpu.make_async_remote_copy(
            src_ref=send.at[v, lax.rem(me + o, n)],
            dst_ref=recv.at[v, o - 1],
            send_sem=send_sem.at[v, o - 1],
            recv_sem=recv_sem.at[v, o - 1],
            device_id=(lax.rem(me + o, n), band),
            device_id_type=MESH,
        )

    def upward(v):
        return pltpu.make_async_remote_copy(
            src_ref=dens.at[v, :, pl.ds(width - trail, trail)],
            dst_ref=top_ref.at[v],
            send_sem=up_sem.at[v, 0],
            recv_sem=up_sem.at[v, 1],
            device_id=(me, band + 1),
            device_id_type=MESH,
        )

    def downward(v):
        return pltpu.make_async_remote_copy(
            src_ref=dens.at[v, :, pl.ds(0, lead)],
            dst_ref=bottom_ref.at[v],
            send_sem=down_sem.at[v, 0],
            recv_sem=down_sem.at[v, 1],
            device_id=(me, band - 1),
            device_id_type=MESH,
        )

    def blank(v, side):
        if side == 0:
            return pltpu.make_async_copy(zeros.at[:, pl.ds(0, trail)], top_ref.at[v], zero_sem.at[0, v])
        return pltpu.make_async_copy(zeros.at[:, pl.ds(0, lead)], bottom_ref.at[v], zero_sem.at[1, v])

    def keep(v):
        return pltpu.make_async_copy(dens.at[v], own_ref.at[v], own_sem.at[v])

    for v in range(items):
        for d, block in regroup(codes_ref, exponents_ref, v, n, cells, width):
            send[v, d] = block
        if v == 0:
            beside = jnp.where(band > 0, 1, 0) + jnp.where(band < count - 1, 1, 0)
            pl.semaphore_wait(barrier, n - 1 + beside)
        if v < AHEAD:
            for o in range(1, n):
                outgoing(v, o).start()

    zeros[...] = jnp.zeros_like(zeros)

    @pl.when(band == 0)
    def _():
        for v in range(items):
            blank(v, 0).start()

    @pl.when(band == count - 1)
    def _():
        for v in range(items):
            blank(v, 1).start()

    def item(v, _):
        wide = widths_ref[v]
        point = lax.broadcasted_iota(jnp.int32, (1, POINTS), 1)
        mag = jnp.where(point >= HALF, point - HALF, point)
        octave = jnp.maximum(mag - 64, 0) >> 6
        mag = jnp.where(mag < 128, mag, (mag - 64 * octave) << octave).astype(jnp.float32)
        value = jnp.where(point >= HALF, -mag, mag) * (1.0 / FINE)
        cross = lax.broadcasted_iota(jnp.int32, (bins, bins), 0) == lax.broadcasted_iota(jnp.int32, (bins, bins), 1)
        center = jnp.sum(jnp.where(cross, centers_ref[pl.ds(v, 1), :], 0.0), axis=1, keepdims=True)
        scaled = (center - value) / wide
        norm = 1.0 / (total * wide * math.sqrt(2.0 * math.pi))
        table[...] = (jnp.exp(-0.5 * scaled * scaled) * norm).astype(jnp.bfloat16)

        for o in range(1, n):
            outgoing(v, o).wait_recv()

        @pl.when(v + AHEAD < items)
        def _():
            for o in range(1, n):
                outgoing(v + AHEAD, o).start()


        for i in range(n):
            if i == 0:
                vals = send[v, me]
            else:
                vals = recv[v, i - 1]
            vals = vals.astype(jnp.float32) * FINE
            size = jnp.abs(vals).astype(jnp.int32)
            octave = jnp.zeros_like(size)
            for limit in (128, 256, 512, 1024):
                octave = octave + jnp.where(size >= limit, 1, 0)
            index = (size >> octave) + 64 * octave + jnp.where(vals < 0, HALF, 0)
            field = (index * (65536 // WORDS + 1)) >> 16
            there = size < 2048
            words[i * members : (i + 1) * members] = jnp.where(there, index - WORDS * field, WORDS)
            steps[i * members : (i + 1) * members] = jnp.left_shift(1, jnp.where(there, 2 * field, 0))

        def finish(low, high):
            part = jnp.dot(table[...], counts[:, low:high], preferred_element_type=jnp.float32)
            dens[v, :, low:high] = part.astype(jnp.bfloat16)

        def group(i, _):
            spot = jnp.where(i < front + back, groups - back + i - front, i - back)
            g = jnp.where(i < front, i, spot)
            at = pl.ds(pl.multiple_of(g * lanes, lanes), lanes)
            row = lax.broadcasted_iota(jnp.int32, (WORDS, lanes), 0)
            for start in range(0, total, 15):
                stop = min(start + 15, total)
                raw = odd = None
                for first in range(start, stop, 3):
                    pair = None
                    for m in range(first, min(first + 3, stop)):
                        one = jnp.where(row == words[m : m + 1, at], steps[m : m + 1, at], 0)
                        pair = one if pair is None else pair + one
                    high = lax.shift_right_logical(pair, 2) & 0x33333333
                    raw = pair if raw is None else raw + pair
                    odd = high if odd is None else odd + high
                even = raw - (odd << 2)
                for k, four in enumerate((even, odd)):
                    low = four & 0x0F0F0F0F
                    high = lax.shift_right_logical(four, 4) & 0x0F0F0F0F
                    if start == 0:
                        bytes4[k] = low
                        bytes4[k + 2] = high
                    else:
                        bytes4[k] += low
                        bytes4[k + 2] += high
            for f in range(FIELDS):
                part = lax.shift_right_logical(bytes4[f % 4], 8 * (f // 4))
                if f // 4 < 3:
                    part = part & 0xFF
                counts[f * WORDS : (f + 1) * WORDS, at] = part.astype(jnp.float32).astype(jnp.bfloat16)
            return 0

        lax.fori_loop(0, front + back, group, 0)
        finish(0, front * lanes)
        finish((groups - back) * lanes, groups * lanes)

        @pl.when(band > 0)
        def _():
            downward(v).start()

        @pl.when(band < count - 1)
        def _():
            upward(v).start()

        if front + back < groups:
            lax.fori_loop(front + back, groups, group, 0)
            finish(front * lanes, (groups - back) * lanes)
        keep(v).start()
        return 0

    lax.fori_loop(0, items, item, 0)

    for v in range(items):
        keep(v).wait()
        for o in range(1, n):
            outgoing(v, o).wait_send()

    @pl.when(band > 0)
    def _():
        for v in range(items):
            downward(v).wait_send()
            upward(v).wait_recv()

    @pl.when(band < count - 1)
    def _():
        for v in range(items):
            upward(v).wait_send()
            downward(v).wait_recv()

    @pl.when(band == 0)
    def _():
        for v in range(items):
            blank(v, 0).wait()

    @pl.when(band == count - 1)
    def _():
        for v in range(items):
            blank(v, 1).wait()


def window_kernel(rows, cells, chunks, own_ref, top_ref, bottom_ref, mix_ref, mix_top_ref, mix_bottom_ref, out_ref):
    edge = mix_top_ref.shape[0]
    dims = (((1,), (1,)), ((), ()))
    def mixed(mix, dens):
        return lax.dot_general(mix, dens, dims, preferred_element_type=jnp.float32)
    above = mixed(mix_top_ref[...], top_ref[0])
    below = mixed(mix_bottom_ref[...], bottom_ref[0])
    for c, (first, low, high) in enumerate(chunks):
        size = mix_ref.shape[1] // cells
        full = mixed(mix_ref[c, :, : high - low], own_ref[0, :, low:high])
        for r in range(first, first + size):
            part = full[(r - first) * cells : (r - first + 1) * cells]
            if r < REACH:
                part = part + above[r * cells : (r + 1) * cells]
            if r >= rows - REACH:
                at = edge - (rows - r) * cells
                part = part + below[at : at + cells]
            out_ref[r, 0] = (part * (1.0 / 25.0)).astype(jnp.bfloat16)


def window(rows, first, cells, lanes, source_rows, source_first):
    wide = cells + 2 * REACH
    out = np.arange(rows * cells)
    row, place = lanes // wide, lanes % wide
    dr = np.abs((out // cells + first)[:, None] - (row + source_first)[None, :])
    dl = place[None, :] - (out % cells)[:, None]
    real = (row >= source_rows[0]) & (row < source_rows[1])
    inside = (dr <= REACH) & (dl >= 0) & (dl <= 2 * REACH) & real[None, :]
    return inside.astype(jnp.bfloat16)


def solution(mesh):
    n = mesh.shape["member"]
    count = mesh.shape["band"]

    def shards(codes, exponents, centers, widths):
        members, rows, items, lon = codes.shape
        bins = centers.shape[1]
        cells = lon // n
        wide = cells + 2 * REACH
        width = -(-rows * wide // 128) * 128
        exponents = jnp.transpose(exponents, (2, 0, 1))
        codes = jnp.transpose(codes, (1, 2, 0, 3))
        lead = -(-REACH * wide // 128) * 128
        trail = width - (rows - REACH) * wide // 128 * 128
        params = pltpu.CompilerParams(vmem_limit_bytes=VMEM)
        vmem = pl.BlockSpec(memory_space=pltpu.VMEM)
        hbm = pl.BlockSpec(memory_space=pl.ANY)
        dens, top, bottom = pl.pallas_call(
            functools.partial(density_kernel, n, count, cells, width, lead, trail),
            in_specs=[vmem, vmem, vmem, pl.BlockSpec(memory_space=pltpu.SMEM)],
            out_specs=[hbm, hbm, hbm],
            out_shape=[
                jax.ShapeDtypeStruct((items, bins, width), jnp.bfloat16),
                jax.ShapeDtypeStruct((items, bins, trail), jnp.bfloat16),
                jax.ShapeDtypeStruct((items, bins, lead), jnp.bfloat16),
            ],
            scratch_shapes=[
                pltpu.VMEM((items, n, members, width), jnp.bfloat16),
                pltpu.VMEM((items, max(n - 1, 1), members, width), jnp.bfloat16),
                pltpu.VMEM((items, bins, width), jnp.bfloat16),
                pltpu.VMEM((bins, max(lead, trail)), jnp.bfloat16),
                pltpu.VMEM((bins, POINTS), jnp.bfloat16),
                pltpu.VMEM((n * members, width), jnp.int32),
                pltpu.VMEM((n * members, width), jnp.int32),
                pltpu.VMEM((POINTS, width), jnp.bfloat16),
                pltpu.VMEM((4, WORDS, 128), jnp.int32),
                pltpu.SemaphoreType.DMA((items, n)),
                pltpu.SemaphoreType.DMA((items, n)),
                pltpu.SemaphoreType.DMA((items, 2)),
                pltpu.SemaphoreType.DMA((items, 2)),
                pltpu.SemaphoreType.DMA((items,)),
                pltpu.SemaphoreType.DMA((2, items)),
            ],
            compiler_params=pltpu.CompilerParams(
                vmem_limit_bytes=VMEM, collective_id=0, has_side_effects=True
            ),
        )(codes, exponents, centers, widths)
        size = max(k for k in (3, 2, 1) if rows % k == 0)
        chunks = []
        for first in range(0, rows, size):
            low = max(first - REACH, 0) * wide // 128 * 128
            high = -(-min(first + size + REACH, rows) * wide // 128) * 128
            chunks.append((first, low, high))
        depth = max(high - low for _, low, high in chunks)
        mix = np.stack(
            [window(size, first, cells, np.arange(low, low + depth), (0, rows), 0) for first, low, _ in chunks]
        )
        mix_top = window(REACH, 0, cells, np.arange(width - trail, width), (rows - REACH, rows), -rows)
        mix_bottom = window(REACH, rows - REACH, cells, np.arange(lead), (0, REACH), rows)
        whole = pl.BlockSpec(memory_space=pltpu.VMEM)
        return pl.pallas_call(
            functools.partial(window_kernel, rows, cells, chunks),
            grid=(items,),
            in_specs=[
                pl.BlockSpec((1, bins, width), lambda v: (v, 0, 0)),
                pl.BlockSpec((1, bins, trail), lambda v: (v, 0, 0)),
                pl.BlockSpec((1, bins, lead), lambda v: (v, 0, 0)),
                whole,
                whole,
                whole,
            ],
            out_specs=pl.BlockSpec((rows, 1, cells, bins), lambda v: (0, v, 0, 0)),
            out_shape=jax.ShapeDtypeStruct((rows, items, cells, bins), jnp.bfloat16),
            compiler_params=params,
        )(dens, top, bottom, mix, mix_top, mix_bottom)

    return jax.shard_map(
        shards,
        mesh=mesh,
        in_specs=(P("member", "band", None, None), P("member", "band", None), P(), P()),
        out_specs=P("band", None, "member", None),
        check_vma=False,
    )
```

```python
import functools
import math

import jax
import jax.numpy as jnp
import numpy as np
from jax import lax
from jax.experimental import pallas as pl
from jax.experimental.pallas import tpu as pltpu
from jax.sharding import PartitionSpec as P

MESH = pl.DeviceIdType.MESH
REACH = 2
FINE = 256.0
OUTSIDE = 16.0
HALF = 384
POINTS = 2 * HALF
FIELDS = 16
WORDS = POINTS // FIELDS
VMEM = 60 * 1024 * 1024
AHEAD = 3


def regroup(codes_ref, exponents_ref, v, n, cells, width):
    rows, _, members, _ = codes_ref.shape
    wide = cells + 2 * REACH
    lon = codes_ref.shape[3]
    edge = jnp.full((members, REACH), OUTSIDE, jnp.float32)
    rest = jnp.full((members, width - rows * wide), OUTSIDE, jnp.float32)
    scale = jnp.left_shift(1, exponents_ref[v] + 8).astype(jnp.float32) * (1.0 / FINE)
    lines = [codes_ref[r, v].astype(jnp.float32) * scale[:, r : r + 1] for r in range(rows)]
    for d in range(n):
        low, high = d * cells - REACH, (d + 1) * cells + REACH
        parts = []
        for line in lines:
            if low < 0:
                parts.append(edge)
            parts.append(line[:, max(low, 0) : min(high, lon)])
            if high > lon:
                parts.append(edge)
        yield d, jnp.concatenate(parts + [rest], axis=1).astype(jnp.bfloat16)


def density_kernel(
    n, count, cells, width, lead, trail,
    codes_ref, exponents_ref, centers_ref, widths_ref,
    own_ref, top_ref, bottom_ref,
    send, recv, dens, zeros, table, words, steps, counts, bytes4,
    send_sem, recv_sem, up_sem, down_sem, own_sem, zero_sem,
):
    rows, items, members, _ = codes_ref.shape
    total = n * members
    bins = centers_ref.shape[1]
    lanes = 128
    groups = width // lanes
    front = lead // lanes
    back = min(trail // lanes, groups - front)
    me = lax.axis_index("member")
    band = lax.axis_index("band")

    barrier = pltpu.get_barrier_semaphore()
    for o in range(1, n):
        pl.semaphore_signal(barrier, inc=1, device_id=(lax.rem(me + o, n), band), device_id_type=MESH)

    @pl.when(band > 0)
    def _():
        pl.semaphore_signal(barrier, inc=1, device_id=(me, band - 1), device_id_type=MESH)

    @pl.when(band < count - 1)
    def _():
        pl.semaphore_signal(barrier, inc=1, device_id=(me, band + 1), device_id_type=MESH)

    def outgoing(v, o):
        return pltpu.make_async_remote_copy(
            src_ref=send.at[v, lax.rem(me + o, n)],
            dst_ref=recv.at[v, o - 1],
            send_sem=send_sem.at[v, o - 1],
            recv_sem=recv_sem.at[v, o - 1],
            device_id=(lax.rem(me + o, n), band),
            device_id_type=MESH,
        )

    def upward(v):
        return pltpu.make_async_remote_copy(
            src_ref=dens.at[v, :, pl.ds(width - trail, trail)],
            dst_ref=top_ref.at[v],
            send_sem=up_sem.at[v, 0],
            recv_sem=up_sem.at[v, 1],
            device_id=(me, band + 1),
            device_id_type=MESH,
        )

    def downward(v):
        return pltpu.make_async_remote_copy(
            src_ref=dens.at[v, :, pl.ds(0, lead)],
            dst_ref=bottom_ref.at[v],
            send_sem=down_sem.at[v, 0],
            recv_sem=down_sem.at[v, 1],
            device_id=(me, band - 1),
            device_id_type=MESH,
        )

    def blank(v, side):
        if side == 0:
            return pltpu.make_async_copy(zeros.at[:, pl.ds(0, trail)], top_ref.at[v], zero_sem.at[0, v])
        return pltpu.make_async_copy(zeros.at[:, pl.ds(0, lead)], bottom_ref.at[v], zero_sem.at[1, v])

    def keep(v):
        return pltpu.make_async_copy(dens.at[v], own_ref.at[v], own_sem.at[v])

    for v in range(items):
        for d, block in regroup(codes_ref, exponents_ref, v, n, cells, width):
            send[v, d] = block
        if v == 0:
            beside = jnp.where(band > 0, 1, 0) + jnp.where(band < count - 1, 1, 0)
            pl.semaphore_wait(barrier, n - 1 + beside)
        if v < AHEAD:
            for o in range(1, n):
                outgoing(v, o).start()

    zeros[...] = jnp.zeros_like(zeros)

    @pl.when(band == 0)
    def _():
        for v in range(items):
            blank(v, 0).start()

    @pl.when(band == count - 1)
    def _():
        for v in range(items):
            blank(v, 1).start()

    def item(v, _):
        wide = widths_ref[v]
        point = lax.broadcasted_iota(jnp.int32, (1, POINTS), 1)
        mag = jnp.where(point >= HALF, point - HALF, point)
        octave = jnp.maximum(mag - 64, 0) >> 6
        mag = jnp.where(mag < 128, mag, (mag - 64 * octave) << octave).astype(jnp.float32)
        value = jnp.where(point >= HALF, -mag, mag) * (1.0 / FINE)
        cross = lax.broadcasted_iota(jnp.int32, (bins, bins), 0) == lax.broadcasted_iota(jnp.int32, (bins, bins), 1)
        center = jnp.sum(jnp.where(cross, centers_ref[pl.ds(v, 1), :], 0.0), axis=1, keepdims=True)
        scaled = (center - value) / wide
        norm = 1.0 / (total * wide * math.sqrt(2.0 * math.pi))
        table[...] = (jnp.exp(-0.5 * scaled * scaled) * norm).astype(jnp.bfloat16)

        for o in range(1, n):
            outgoing(v, o).wait_recv()

        @pl.when(v + AHEAD < items)
        def _():
            for o in range(1, n):
                outgoing(v + AHEAD, o).start()


        for i in range(n):
            if i == 0:
                vals = send[v, me]
            else:
                vals = recv[v, i - 1]
            vals = vals.astype(jnp.float32) * FINE
            size = jnp.abs(vals).astype(jnp.int32)
            octave = jnp.zeros_like(size)
            for limit in (128, 256, 512, 1024):
                octave = octave + jnp.where(size >= limit, 1, 0)
            index = (size >> octave) + 64 * octave + jnp.where(vals < 0, HALF, 0)
            field = (index * (65536 // WORDS + 1)) >> 16
            there = size < 2048
            words[i * members : (i + 1) * members] = jnp.where(there, index - WORDS * field, WORDS)
            steps[i * members : (i + 1) * members] = jnp.left_shift(1, jnp.where(there, 2 * field, 0))

        def finish(low, high):
            part = jnp.dot(table[...], counts[:, low:high], preferred_element_type=jnp.float32)
            dens[v, :, low:high] = part.astype(jnp.bfloat16)

        def group(i, _):
            spot = jnp.where(i < front + back, groups - back + i - front, i - back)
            g = jnp.where(i < front, i, spot)
            at = pl.ds(pl.multiple_of(g * lanes, lanes), lanes)
            row = lax.broadcasted_iota(jnp.int32, (WORDS, lanes), 0)
            for start in range(0, total, 15):
                stop = min(start + 15, total)
                raw = odd = None
                for first in range(start, stop, 3):
                    pair = None
                    for m in range(first, min(first + 3, stop)):
                        one = jnp.where(row == words[m : m + 1, at], steps[m : m + 1, at], 0)
                        pair = one if pair is None else pair + one
                    high = lax.shift_right_logical(pair, 2) & 0x33333333
                    raw = pair if raw is None else raw + pair
                    odd = high if odd is None else odd + high
                even = raw - (odd << 2)
                for k, four in enumerate((even, odd)):
                    low = four & 0x0F0F0F0F
                    high = lax.shift_right_logical(four, 4) & 0x0F0F0F0F
                    if start == 0:
                        bytes4[k] = low
                        bytes4[k + 2] = high
                    else:
                        bytes4[k] += low
                        bytes4[k + 2] += high
            for f in range(FIELDS):
                part = lax.shift_right_logical(bytes4[f % 4], 8 * (f // 4))
                if f // 4 < 3:
                    part = part & 0xFF
                counts[f * WORDS : (f + 1) * WORDS, at] = part.astype(jnp.float32).astype(jnp.bfloat16)
            return 0

        lax.fori_loop(0, front + back, group, 0, unroll=2)
        finish(0, front * lanes)
        finish((groups - back) * lanes, groups * lanes)

        @pl.when(band > 0)
        def _():
            downward(v).start()

        @pl.when(band < count - 1)
        def _():
            upward(v).start()

        if front + back < groups:
            lax.fori_loop(front + back, groups, group, 0)
            finish(front * lanes, (groups - back) * lanes)
        keep(v).start()
        return 0

    lax.fori_loop(0, items, item, 0)

    for v in range(items):
        keep(v).wait()
        for o in range(1, n):
            outgoing(v, o).wait_send()

    @pl.when(band > 0)
    def _():
        for v in range(items):
            downward(v).wait_send()
            upward(v).wait_recv()

    @pl.when(band < count - 1)
    def _():
        for v in range(items):
            upward(v).wait_send()
            downward(v).wait_recv()

    @pl.when(band == 0)
    def _():
        for v in range(items):
            blank(v, 0).wait()

    @pl.when(band == count - 1)
    def _():
        for v in range(items):
            blank(v, 1).wait()


def window_kernel(rows, cells, chunks, own_ref, top_ref, bottom_ref, mix_ref, mix_top_ref, mix_bottom_ref, out_ref):
    edge = mix_top_ref.shape[0]
    dims = (((1,), (1,)), ((), ()))
    def mixed(mix, dens):
        return lax.dot_general(mix, dens, dims, preferred_element_type=jnp.float32)
    above = mixed(mix_top_ref[...], top_ref[0])
    below = mixed(mix_bottom_ref[...], bottom_ref[0])
    for c, (first, low, high) in enumerate(chunks):
        size = mix_ref.shape[1] // cells
        full = mixed(mix_ref[c, :, : high - low], own_ref[0, :, low:high])
        for r in range(first, first + size):
            part = full[(r - first) * cells : (r - first + 1) * cells]
            if r < REACH:
                part = part + above[r * cells : (r + 1) * cells]
            if r >= rows - REACH:
                at = edge - (rows - r) * cells
                part = part + below[at : at + cells]
            out_ref[r, 0] = (part * (1.0 / 25.0)).astype(jnp.bfloat16)


def window(rows, first, cells, lanes, source_rows, source_first):
    wide = cells + 2 * REACH
    out = np.arange(rows * cells)
    row, place = lanes // wide, lanes % wide
    dr = np.abs((out // cells + first)[:, None] - (row + source_first)[None, :])
    dl = place[None, :] - (out % cells)[:, None]
    real = (row >= source_rows[0]) & (row < source_rows[1])
    inside = (dr <= REACH) & (dl >= 0) & (dl <= 2 * REACH) & real[None, :]
    return inside.astype(jnp.bfloat16)


def solution(mesh):
    n = mesh.shape["member"]
    count = mesh.shape["band"]

    def shards(codes, exponents, centers, widths):
        members, rows, items, lon = codes.shape
        bins = centers.shape[1]
        cells = lon // n
        wide = cells + 2 * REACH
        width = -(-rows * wide // 128) * 128
        exponents = jnp.transpose(exponents, (2, 0, 1))
        codes = jnp.transpose(codes, (1, 2, 0, 3))
        lead = -(-REACH * wide // 128) * 128
        trail = width - (rows - REACH) * wide // 128 * 128
        params = pltpu.CompilerParams(vmem_limit_bytes=VMEM)
        vmem = pl.BlockSpec(memory_space=pltpu.VMEM)
        hbm = pl.BlockSpec(memory_space=pl.ANY)
        dens, top, bottom = pl.pallas_call(
            functools.partial(density_kernel, n, count, cells, width, lead, trail),
            in_specs=[vmem, vmem, vmem, pl.BlockSpec(memory_space=pltpu.SMEM)],
            out_specs=[hbm, hbm, hbm],
            out_shape=[
                jax.ShapeDtypeStruct((items, bins, width), jnp.bfloat16),
                jax.ShapeDtypeStruct((items, bins, trail), jnp.bfloat16),
                jax.ShapeDtypeStruct((items, bins, lead), jnp.bfloat16),
            ],
            scratch_shapes=[
                pltpu.VMEM((items, n, members, width), jnp.bfloat16),
                pltpu.VMEM((items, max(n - 1, 1), members, width), jnp.bfloat16),
                pltpu.VMEM((items, bins, width), jnp.bfloat16),
                pltpu.VMEM((bins, max(lead, trail)), jnp.bfloat16),
                pltpu.VMEM((bins, POINTS), jnp.bfloat16),
                pltpu.VMEM((n * members, width), jnp.int32),
                pltpu.VMEM((n * members, width), jnp.int32),
                pltpu.VMEM((POINTS, width), jnp.bfloat16),
                pltpu.VMEM((4, WORDS, 128), jnp.int32),
                pltpu.SemaphoreType.DMA((items, n)),
                pltpu.SemaphoreType.DMA((items, n)),
                pltpu.SemaphoreType.DMA((items, 2)),
                pltpu.SemaphoreType.DMA((items, 2)),
                pltpu.SemaphoreType.DMA((items,)),
                pltpu.SemaphoreType.DMA((2, items)),
            ],
            compiler_params=pltpu.CompilerParams(
                vmem_limit_bytes=VMEM, collective_id=0, has_side_effects=True
            ),
        )(codes, exponents, centers, widths)
        size = max(k for k in (3, 2, 1) if rows % k == 0)
        chunks = []
        for first in range(0, rows, size):
            low = max(first - REACH, 0) * wide // 128 * 128
            high = -(-min(first + size + REACH, rows) * wide // 128) * 128
            chunks.append((first, low, high))
        depth = max(high - low for _, low, high in chunks)
        mix = np.stack(
            [window(size, first, cells, np.arange(low, low + depth), (0, rows), 0) for first, low, _ in chunks]
        )
        mix_top = window(REACH, 0, cells, np.arange(width - trail, width), (rows - REACH, rows), -rows)
        mix_bottom = window(REACH, rows - REACH, cells, np.arange(lead), (0, REACH), rows)
        whole = pl.BlockSpec(memory_space=pltpu.VMEM)
        return pl.pallas_call(
            functools.partial(window_kernel, rows, cells, chunks),
            grid=(items,),
            in_specs=[
                pl.BlockSpec((1, bins, width), lambda v: (v, 0, 0)),
                pl.BlockSpec((1, bins, trail), lambda v: (v, 0, 0)),
                pl.BlockSpec((1, bins, lead), lambda v: (v, 0, 0)),
                whole,
                whole,
                whole,
            ],
            out_specs=pl.BlockSpec((rows, 1, cells, bins), lambda v: (0, v, 0, 0)),
            out_shape=jax.ShapeDtypeStruct((rows, items, cells, bins), jnp.bfloat16),
            compiler_params=params,
        )(dens, top, bottom, mix, mix_top, mix_bottom)

    return jax.shard_map(
        shards,
        mesh=mesh,
        in_specs=(P("member", "band", None, None), P("member", "band", None), P(), P()),
        out_specs=P("band", None, "member", None),
        check_vma=False,
    )
```
